32 devices in a mesh: row: 8 (over z, y), col: 4 (over x, core).
Axes of the slice: x: 2, y: 2, z: 4, core: 2. Of those that a mesh axis runs over, the one named last changes fastest.
Arguments:
- interaction: bfloat16 [8192, 8192], P('row', 'col'), may hold values from -0.0625 to 0.0625
- amplitudes: bfloat16 [8192, 8192], P('row', 'col'), may hold values from -6 to 6
- driver: bfloat16 [8192, 8192], P('row', 'col'), may hold values from -6 to 6
- dressing: bfloat16 [1024, 1024], replicated, may hold values from -0.1875 to 0.1875
- occ_energy: float32 [8], replicated, may hold values from -2 to -0.5
- vir_energy: float32 [1024], replicated, may hold values from 0.5 to 3
Outputs:
- updated: float32 [8192, 8192], P('row', 'col')
The draws below stay inside these ranges and needn't reach their ends.
All inputs are finite; a program needn't handle non-finite values.
Results may differ from the reference program's by a relative error of at most 0.00084.
Values may be sent and summed in bfloat16 or wider, within the bound.
A program may use at most 128 MiB of HBM per device.

```python
import jax
import jax.numpy as jnp

V = 1024
OCC = 8
K = 8192
ROWS = 8192
COLUMNS = 8192


def level_of(stream_key, dims, cuts, low, top_value):
    loudness, own = 1.0, jax.random.fold_in(stream_key, 6)
    for position, parts in cuts:
        heights = jnp.exp(jax.random.uniform(jax.random.fold_in(own, position), (parts,), jnp.float32, low / len(cuts), top_value / len(cuts)))
        loudness = loudness * jnp.repeat(heights, dims[position] // parts).reshape([-1 if axis == position else 1 for axis in range(len(dims))])
    return loudness


def centred(key, dims, deviation, reach, shards=(), kind=jnp.bfloat16):
    entries = deviation * jax.random.normal(key, dims, jnp.float32)
    if shards:
        entries = entries * level_of(key, dims, shards, -0.22, 0.18)
    return jnp.clip(entries, -reach, reach).astype(kind)


def setup_inputs(seed: int = 0) -> dict:
    keys = jax.random.split(jax.random.key(seed), 7)
    interaction = centred(keys[0], (ROWS, K), K ** -0.5, 0.0625, ((0, 8), (1, 4)))
    amplitudes = centred(keys[1], (K, COLUMNS), 1.0, 6.0, ((0, 8), (1, 4)))
    driver = centred(keys[2], (ROWS, COLUMNS), 1.0, 6.0, ((0, 8), (1, 4)))
    dressing = centred(keys[3], (V, V), V ** -0.5, 0.1875)
    occ_energy = jnp.clip(jax.random.uniform(keys[4], (OCC,), jnp.float32, -2.0, -0.5), -2.0, -0.5)
    vir_energy = jnp.clip(jax.random.uniform(keys[5], (V,), jnp.float32, 0.5, 3.0), 0.5, 3.0)
    return dict(interaction=interaction, amplitudes=amplitudes, driver=driver, dressing=dressing, occ_energy=occ_energy, vir_energy=vir_energy)


def reference(interaction, amplitudes, driver, dressing, occ_energy, vir_energy):
    cycle_term = jnp.dot(interaction, amplitudes, preferred_element_type=jnp.float32)
    line_energy = jnp.repeat(occ_energy, V) - jnp.tile(vir_energy, OCC)
    denominator = line_energy[:, None] + line_energy[None, :]
    summed = driver.astype(jnp.float32) + cycle_term
    first_order = (summed / denominator).astype(jnp.bfloat16)
    flattened = first_order.reshape(ROWS * OCC, V)
    dressed = jnp.dot(flattened, dressing, preferred_element_type=jnp.float32)
    dressed = dressed.reshape(ROWS, COLUMNS).astype(jnp.bfloat16)
    return (summed + dressed.astype(jnp.float32)) / denominator
```

```python
import jax
import jax.numpy as jnp
from jax import lax
from jax.sharding import PartitionSpec as P


def ring_owner(position, count):
    return jnp.where(position < count // 2, 2 * position, 2 * (count - 1 - position) + 1)


def ring_position(index, count):
    return jnp.where(index % 2 == 0, index // 2, count - 1 - index // 2)


def line_energy(occupied, virtual, offset, length):
    orbitals = virtual.shape[0]
    energy = jnp.repeat(occupied, orbitals) - jnp.tile(virtual, occupied.shape[0])
    return lax.dynamic_slice_in_dim(energy, offset, length)


def dress(first_order, dressing):
    orbitals = dressing.shape[0]
    rows, columns = first_order.shape
    if columns % orbitals == 0:
        parts = [
            jnp.dot(first_order[:, j : j + orbitals], dressing, preferred_element_type=jnp.float32).astype(jnp.bfloat16)
            for j in range(0, columns, orbitals)
        ]
        return jnp.concatenate(parts, axis=1)
    lines = lax.all_to_all(first_order, "col", split_axis=0, concat_axis=1, tiled=True)
    line_rows, line_columns = lines.shape
    flattened = lines.reshape(line_rows * (line_columns // orbitals), orbitals)
    dressed_lines = jnp.dot(flattened, dressing, preferred_element_type=jnp.float32)
    dressed_lines = dressed_lines.reshape(line_rows, line_columns).astype(jnp.bfloat16)
    return lax.all_to_all(dressed_lines, "col", split_axis=1, concat_axis=0, tiled=True)


def cycle(interaction, amplitudes, count):
    order = list(range(0, count, 2)) + list(range(count - 1, 0, -2))
    up = [(order[p], order[(p + 1) % count]) for p in range(count)]
    down = [(b, a) for a, b in up]
    panel = lax.all_gather(interaction, "col", axis=1, tiled=True)
    depth = amplitudes.shape[0]
    half = depth // 2
    place = ring_position(lax.axis_index("row"), count)
    total = None
    waiting = []
    high, low = amplitudes[:half], amplitudes[half:]
    for step in range(count):
        if step < count - 1:
            next_high = lax.ppermute(high, "row", up)
            next_low = lax.ppermute(low, "row", down)
        waiting += [(high, place - step, 0), (low, place + step, half)]
        for block, position, shift in waiting if step >= 2 else ():
            owner = ring_owner((position + count) % count, count)
            part = lax.dynamic_slice_in_dim(panel, owner * depth + shift, half, axis=1)
            term = jnp.dot(part, block, preferred_element_type=jnp.float32)
            total = term if total is None else total + term
        if step >= 2:
            waiting = []
            next_high, next_low, total = lax.optimization_barrier((next_high, next_low, total))
        else:
            next_high, next_low = lax.optimization_barrier((next_high, next_low))
        high, low = next_high, next_low
    return total


def solution(mesh):
    count = mesh.shape["row"]

    def on_device(interaction, amplitudes, driver, dressing, occ_energy, vir_energy):
        row_count, column_count = driver.shape
        cycle_term = cycle(interaction, amplitudes, count)
        row_energy = line_energy(occ_energy, vir_energy, lax.axis_index("row") * row_count, row_count)
        column_energy = line_energy(occ_energy, vir_energy, lax.axis_index("col") * column_count, column_count)
        denominator = row_energy[:, None] + column_energy[None, :]
        summed = driver.astype(jnp.float32) + cycle_term
        first_order = (summed / denominator).astype(jnp.bfloat16)
        dressed = dress(first_order, dressing)
        return (summed + dressed.astype(jnp.float32)) / denominator

    return jax.shard_map(
        on_device,
        mesh=mesh,
        in_specs=(P("row", "col"), P("row", "col"), P("row", "col"), P(), P(), P()),
        out_specs=P("row", "col"),
        check_vma=False,
    )
```

```python
import functools

import jax
import jax.numpy as jnp
from jax import lax
from jax.experimental import pallas as pl
from jax.experimental.pallas import tpu as pltpu
from jax.sharding import PartitionSpec as P


def ring_owner(position, count):
    return jnp.where(position < count // 2, 2 * position, 2 * (count - 1 - position) + 1)


def ring_position(index, count):
    return jnp.where(index % 2 == 0, index // 2, count - 1 - index // 2)


def line_energy(occupied, virtual, offset, length):
    orbitals = virtual.shape[0]
    energy = jnp.repeat(occupied, orbitals) - jnp.tile(virtual, occupied.shape[0])
    return lax.dynamic_slice_in_dim(energy, offset, length)


def dress(first_order, dressing):
    orbitals = dressing.shape[0]
    rows, columns = first_order.shape
    if columns % orbitals == 0:
        parts = [
            jnp.dot(first_order[:, j : j + orbitals], dressing, preferred_element_type=jnp.float32).astype(jnp.bfloat16)
            for j in range(0, columns, orbitals)
        ]
        return jnp.concatenate(parts, axis=1)
    lines = lax.all_to_all(first_order, "col", split_axis=0, concat_axis=1, tiled=True)
    line_rows, line_columns = lines.shape
    flattened = lines.reshape(line_rows * (line_columns // orbitals), orbitals)
    dressed_lines = jnp.dot(flattened, dressing, preferred_element_type=jnp.float32)
    dressed_lines = dressed_lines.reshape(line_rows, line_columns).astype(jnp.bfloat16)
    return lax.all_to_all(dressed_lines, "col", split_axis=1, concat_axis=0, tiled=True)


def cycle(interaction, amplitudes, count):
    order = list(range(0, count, 2)) + list(range(count - 1, 0, -2))
    up = [(order[p], order[(p + 1) % count]) for p in range(count)]
    down = [(b, a) for a, b in up]
    panel = lax.all_gather(interaction, "col", axis=1, tiled=True)
    depth = amplitudes.shape[0]
    half = depth // 2
    place = ring_position(lax.axis_index("row"), count)
    total = None
    waiting = []
    high, low = amplitudes[:half], amplitudes[half:]
    for step in range(count):
        if step < count - 1:
            next_high = lax.ppermute(high, "row", up)
            next_low = lax.ppermute(low, "row", down)
        waiting += [(high, place - step, 0), (low, place + step, half)]
        for block, position, shift in waiting if step >= 2 else ():
            owner = ring_owner((position + count) % count, count)
            part = lax.dynamic_slice_in_dim(panel, owner * depth + shift, half, axis=1)
            term = jnp.dot(part, block, preferred_element_type=jnp.float32)
            total = term if total is None else total + term
        if step >= 2:
            waiting = []
            next_high, next_low, total = lax.optimization_barrier((next_high, next_low, total))
        else:
            next_high, next_low = lax.optimization_barrier((next_high, next_low))
        high, low = next_high, next_low
    return total


MESH = pl.DeviceIdType.MESH
SUBS = 4


def ring_kernel(
    count, cols, lines, amplitudes, interaction, driver, dressing, row_energy, column_energy, out,
    land, panel, total, driver_line, operator, send_sem, recv_sem, w_send, w_recv, own_sem, local_sem,
):
    row, col = lax.axis_index("row"), lax.axis_index("col")
    place = jnp.where(lax.rem(row, 2) == 0, lax.div(row, 2), count - 1 - lax.div(row, 2))
    up = ring_owner(lax.rem(place + 1, count), count)
    down = ring_owner(lax.rem(place + count - 1, count), count)
    sibling = col + 1 - 2 * lax.rem(col, 2)
    half, width = land.shape[2], land.shape[3]
    depth = 2 * half
    per = panel.shape[2] // depth
    orbitals = operator.shape[0]
    group = count * SUBS
    slots = lines * group
    chips = cols // 2
    events = slots - lines * SUBS
    start = events - slots // 2

    barrier = pltpu.get_barrier_semaphore()
    partners = [(up, col), (down, col), (row, sibling)]
    partners += [(row, lax.rem(col + 2 * k, cols)) for k in range(1, chips)]
    for partner in partners:
        pl.semaphore_signal(barrier, inc=1, device_id=partner, device_id_type=MESH)
    pl.semaphore_wait(barrier, len(partners))

    def hop(way, source, slot):
        return pltpu.make_async_remote_copy(
            src_ref=source, dst_ref=land.at[way, slot], send_sem=send_sem.at[way, slot],
            recv_sem=recv_sem.at[way, slot], device_id=((up, down)[way], col), device_id_type=MESH,
        )

    def own_block(way, line, sub):
        return amplitudes.at[pl.ds(way * half, half), pl.ds(line * orbitals + sub * width, width)]

    for sub in range(SUBS):
        for way in range(2):
            hop(way, own_block(way, 0, sub), SUBS + sub).start()

    def w_copy(index, source, slot, target):
        return pltpu.make_async_remote_copy(
            src_ref=source, dst_ref=panel.at[slot], send_sem=w_send.at[index],
            recv_sem=w_recv.at[index], device_id=(row, target), device_id_type=MESH,
        )

    def from_chip(k):
        return lax.rem(col + cols - 2 * k, cols)

    for k in range(1, chips):
        w_copy(2 * k - 1, interaction, col, lax.rem(col + 2 * k, cols)).start()
    w_copy(0, interaction, col, sibling).start()

    own_copies = [
        pltpu.make_async_copy(own_block(way, line, sub), land.at[way, line * group + sub], own_sem.at[way, line * SUBS + sub])
        for line in range(lines) for sub in range(SUBS) for way in range(2)
    ]
    own_copies.append(pltpu.make_async_copy(interaction, panel.at[col], local_sem.at[0]))
    own_copies.append(pltpu.make_async_copy(dressing, operator, local_sem.at[1]))
    for copy in own_copies:
        copy.start()

    def load_driver(line):
        return pltpu.make_async_copy(
            driver.at[:, pl.ds(pl.multiple_of(line * orbitals, orbitals), orbitals)], driver_line, local_sem.at[2]
        )

    def write_line(line):
        return pltpu.make_async_copy(
            total, out.at[:, pl.ds(pl.multiple_of(line * orbitals, orbitals), orbitals)], local_sem.at[3]
        )

    load_driver(0).start()
    for copy in own_copies:
        copy.wait()

    def begin_line(line):
        @pl.when(line > 0)
        def _():
            write_line(line - 1).wait()

        load_driver(line).wait()
        total[...] = driver_line[...].astype(jnp.float32)

        @pl.when(line + 1 < lines)
        def _():
            load_driver(line + 1).start()

    tile = total.shape[0] // 4

    def end_line(line):
        @pl.loop(0, 4)
        def _(index):
            rows = pl.ds(pl.multiple_of(index * tile, tile), tile)
            summed = total[rows, :]
            denominator = row_energy[rows, :] + column_energy[pl.ds(line, 1), :]
            first_order = (summed / denominator).astype(jnp.bfloat16)
            dressed = jnp.dot(first_order, operator[...], preferred_element_type=jnp.float32).astype(jnp.bfloat16)
            total[rows, :] = (summed + dressed.astype(jnp.float32)) / denominator

        write_line(line).start()

    def multiply(item):
        line, within = lax.div(item, group), lax.rem(item, group)
        step, sub = lax.div(within, SUBS), lax.rem(within, SUBS)

        @pl.when(within == 0)
        def _():
            begin_line(line)

        def term(way, position):
            owner = ring_owner(lax.rem(position + count, count), count)
            columns = pl.ds(pl.multiple_of(lax.rem(owner, per) * depth + way * half, half), half)
            return jnp.dot(
                panel[lax.div(owner, per), :, columns], land[way, item], preferred_element_type=jnp.float32
            )

        place_columns = pl.ds(pl.multiple_of(sub * width, width), width)
        total[:, place_columns] += term(0, place - step) + term(1, place + step)

        @pl.when(within == group - 1)
        def _():
            end_line(line)

    @pl.loop(0, events)
    def _(event):
        line = lax.div(event, group - SUBS)
        slot = event + SUBS * (line + 1)
        last = lax.rem(slot, group) >= group - SUBS
        source = jnp.where(last, slot + SUBS, slot)
        for way in range(2):
            hop(way, land.at[way, slot], slot).wait_recv()

            @pl.when(source + SUBS < slots)
            def _():
                hop(way, land.at[way, source], source + SUBS).start()

        @pl.when(event == start * 3 // 4)
        def _():
            for k in range(1, chips):
                origin = from_chip(k)
                w_copy(2 * k - 1, panel.at[origin], origin, sibling).wait_recv()
                w_copy(2 * k, panel.at[origin], origin, sibling).start()

        @pl.when(event == start)
        def _():
            w_copy(0, interaction, sibling, sibling).wait_recv()
            for k in range(1, chips):
                origin = lax.rem(sibling + cols - 2 * k, cols)
                w_copy(2 * k, panel.at[origin], origin, sibling).wait_recv()

        @pl.when(event >= start)
        def _():
            @pl.loop(0, 2)
            def _(which):
                multiply(2 * (event - start) + which)

    write_line(lines - 1).wait()

    @pl.loop(0, events)
    def _(event):
        slot = event + SUBS * (lax.div(event, group - SUBS) + 1)
        for way in range(2):
            hop(way, land.at[way, slot], slot).wait_send()

    w_copy(0, interaction, col, sibling).wait_send()
    for k in range(1, chips):
        w_copy(2 * k - 1, interaction, col, sibling).wait_send()
        origin = from_chip(k)
        w_copy(2 * k, panel.at[origin], origin, sibling).wait_send()


def whole_lines(mesh, interaction, amplitudes, driver, dressing, row_energy, column_energy):
    count, cols = mesh.shape["row"], mesh.shape["col"]
    rows, columns = driver.shape
    depth = amplitudes.shape[0]
    orbitals = dressing.shape[0]
    lines = columns // orbitals
    slots = lines * count * SUBS
    dma = pltpu.SemaphoreType.DMA
    anywhere = pl.BlockSpec(memory_space=pl.ANY)
    vmem = pl.BlockSpec(memory_space=pltpu.VMEM)
    return pl.pallas_call(
        functools.partial(ring_kernel, count, cols, lines),
        out_shape=jax.ShapeDtypeStruct((rows, columns), jnp.float32),
        in_specs=[anywhere] * 4 + [vmem] * 2,
        out_specs=anywhere,
        scratch_shapes=[
            pltpu.VMEM((2, slots, depth // 2, orbitals // SUBS), jnp.bfloat16),
            pltpu.VMEM((cols,) + interaction.shape, jnp.bfloat16),
            pltpu.VMEM((rows, orbitals), jnp.float32),
            pltpu.VMEM((rows, orbitals), jnp.bfloat16),
            pltpu.VMEM(dressing.shape, jnp.bfloat16),
            dma((2, slots)),
            dma((2, slots)),
            dma((cols - 1,)),
            dma((cols - 1,)),
            dma((2, lines * SUBS)),
            dma((4,)),
        ],
        compiler_params=pltpu.CompilerParams(
            collective_id=0, has_side_effects=True, vmem_limit_bytes=62 * 1024 * 1024
        ),
        cost_estimate=pl.CostEstimate(
            flops=2 * rows * columns * (depth * count + orbitals), bytes_accessed=2 * rows * columns * 10, transcendentals=0
        ),
    )(amplitudes, interaction, driver, dressing, row_energy[:, None], column_energy.reshape(lines, orbitals))


def solution(mesh):
    count = mesh.shape["row"]

    def on_device(interaction, amplitudes, driver, dressing, occ_energy, vir_energy):
        row_count, column_count = driver.shape
        row_energy = line_energy(occ_energy, vir_energy, lax.axis_index("row") * row_count, row_count)
        column_energy = line_energy(occ_energy, vir_energy, lax.axis_index("col") * column_count, column_count)
        if column_count % dressing.shape[0] == 0:
            return whole_lines(mesh, interaction, amplitudes, driver, dressing, row_energy, column_energy)
        cycle_term = cycle(interaction, amplitudes, count)
        denominator = row_energy[:, None] + column_energy[None, :]
        summed = driver.astype(jnp.float32) + cycle_term
        first_order = (summed / denominator).astype(jnp.bfloat16)
        dressed = dress(first_order, dressing)
        return (summed + dressed.astype(jnp.float32)) / denominator

    return jax.shard_map(
        on_device,
        mesh=mesh,
        in_specs=(P("row", "col"), P("row", "col"), P("row", "col"), P(), P(), P()),
        out_specs=P("row", "col"),
        check_vma=False,
    )
```

```python
import functools

import jax
import jax.numpy as jnp
from jax import lax
from jax.experimental import pallas as pl
from jax.experimental.pallas import tpu as pltpu
from jax.sharding import PartitionSpec as P


def ring_owner(position, count):
    return jnp.where(position < count // 2, 2 * position, 2 * (count - 1 - position) + 1)


def ring_position(index, count):
    return jnp.where(index % 2 == 0, index // 2, count - 1 - index // 2)


def line_energy(occupied, virtual, offset, length):
    orbitals = virtual.shape[0]
    energy = jnp.repeat(occupied, orbitals) - jnp.tile(virtual, occupied.shape[0])
    return lax.dynamic_slice_in_dim(energy, offset, length)


def dress(first_order, dressing):
    orbitals = dressing.shape[0]
    rows, columns = first_order.shape
    if columns % orbitals == 0:
        parts = [
            jnp.dot(first_order[:, j : j + orbitals], dressing, preferred_element_type=jnp.float32).astype(jnp.bfloat16)
            for j in range(0, columns, orbitals)
        ]
        return jnp.concatenate(parts, axis=1)
    lines = lax.all_to_all(first_order, "col", split_axis=0, concat_axis=1, tiled=True)
    line_rows, line_columns = lines.shape
    flattened = lines.reshape(line_rows * (line_columns // orbitals), orbitals)
    dressed_lines = jnp.dot(flattened, dressing, preferred_element_type=jnp.float32)
    dressed_lines = dressed_lines.reshape(line_rows, line_columns).astype(jnp.bfloat16)
    return lax.all_to_all(dressed_lines, "col", split_axis=1, concat_axis=0, tiled=True)


def cycle(interaction, amplitudes, count):
    order = list(range(0, count, 2)) + list(range(count - 1, 0, -2))
    up = [(order[p], order[(p + 1) % count]) for p in range(count)]
    down = [(b, a) for a, b in up]
    panel = lax.all_gather(interaction, "col", axis=1, tiled=True)
    depth = amplitudes.shape[0]
    half = depth // 2
    place = ring_position(lax.axis_index("row"), count)
    total = None
    waiting = []
    high, low = amplitudes[:half], amplitudes[half:]
    for step in range(count):
        if step < count - 1:
            next_high = lax.ppermute(high, "row", up)
            next_low = lax.ppermute(low, "row", down)
        waiting += [(high, place - step, 0), (low, place + step, half)]
        for block, position, shift in waiting if step >= 2 else ():
            owner = ring_owner((position + count) % count, count)
            part = lax.dynamic_slice_in_dim(panel, owner * depth + shift, half, axis=1)
            term = jnp.dot(part, block, preferred_element_type=jnp.float32)
            total = term if total is None else total + term
        if step >= 2:
            waiting = []
            next_high, next_low, total = lax.optimization_barrier((next_high, next_low, total))
        else:
            next_high, next_low = lax.optimization_barrier((next_high, next_low))
        high, low = next_high, next_low
    return total


MESH = pl.DeviceIdType.MESH
SUBS = 4


def ring_kernel(
    count, cols, lines, amplitudes, interaction, driver, dressing, row_energy, column_energy, out,
    land, panel, total, driver_line, operator, send_sem, recv_sem, w_send, w_recv, own_sem, local_sem,
):
    row, col = lax.axis_index("row"), lax.axis_index("col")
    place = jnp.where(lax.rem(row, 2) == 0, lax.div(row, 2), count - 1 - lax.div(row, 2))
    up = ring_owner(lax.rem(place + 1, count), count)
    down = ring_owner(lax.rem(place + count - 1, count), count)
    sibling = col + 1 - 2 * lax.rem(col, 2)
    half, width = land.shape[2], land.shape[3]
    depth = 2 * half
    per = panel.shape[2] // depth
    orbitals = operator.shape[0]
    group = count * SUBS
    slots = lines * group
    chips = cols // 2
    events = slots - lines * SUBS
    start = events - slots // 2

    barrier = pltpu.get_barrier_semaphore()
    partners = [(up, col), (down, col), (row, sibling)]
    partners += [(row, lax.rem(col + 2 * k, cols)) for k in range(1, chips)]
    for partner in partners:
        pl.semaphore_signal(barrier, inc=1, device_id=partner, device_id_type=MESH)
    pl.semaphore_wait(barrier, len(partners))

    def hop(way, source, slot):
        return pltpu.make_async_remote_copy(
            src_ref=source, dst_ref=land.at[way, slot], send_sem=send_sem.at[way, slot],
            recv_sem=recv_sem.at[way, slot], device_id=((up, down)[way], col), device_id_type=MESH,
        )

    def own_block(way, line, sub):
        return amplitudes.at[pl.ds(way * half, half), pl.ds(line * orbitals + sub * width, width)]

    for sub in range(SUBS):
        for way in range(2):
            hop(way, own_block(way, 0, sub), SUBS + sub).start()

    def w_copy(index, source, slot, target):
        return pltpu.make_async_remote_copy(
            src_ref=source, dst_ref=panel.at[slot], send_sem=w_send.at[index],
            recv_sem=w_recv.at[index], device_id=(row, target), device_id_type=MESH,
        )

    def from_chip(k):
        return lax.rem(col + cols - 2 * k, cols)

    for k in range(1, chips):
        w_copy(2 * k - 1, interaction, col, lax.rem(col + 2 * k, cols)).start()
    w_copy(0, interaction, col, sibling).start()

    own_copies = [
        pltpu.make_async_copy(own_block(way, line, sub), land.at[way, line * group + sub], own_sem.at[way, line * SUBS + sub])
        for line in range(lines) for sub in range(SUBS) for way in range(2)
    ]
    own_copies.append(pltpu.make_async_copy(interaction, panel.at[col], local_sem.at[0]))
    own_copies.append(pltpu.make_async_copy(dressing, operator, local_sem.at[1]))
    for copy in own_copies:
        copy.start()

    def load_driver(line):
        return pltpu.make_async_copy(
            driver.at[:, pl.ds(pl.multiple_of(line * orbitals, orbitals), orbitals)], driver_line, local_sem.at[2]
        )

    def write_line(line):
        return pltpu.make_async_copy(
            total, out.at[:, pl.ds(pl.multiple_of(line * orbitals, orbitals), orbitals)], local_sem.at[3]
        )

    load_driver(0).start()
    for copy in own_copies:
        copy.wait()

    def begin_line(line):
        @pl.when(line > 0)
        def _():
            write_line(line - 1).wait()

        load_driver(line).wait()
        total[...] = driver_line[...].astype(jnp.float32)

        @pl.when(line + 1 < lines)
        def _():
            load_driver(line + 1).start()

    tile = total.shape[0] // 4

    def end_line(line):
        @pl.loop(0, 4)
        def _(index):
            rows = pl.ds(pl.multiple_of(index * tile, tile), tile)
            summed = total[rows, :]
            denominator = row_energy[rows, :] + column_energy[pl.ds(line, 1), :]
            first_order = (summed / denominator).astype(jnp.bfloat16)
            dressed = jnp.dot(first_order, operator[...], preferred_element_type=jnp.float32).astype(jnp.bfloat16)
            total[rows, :] = (summed + dressed.astype(jnp.float32)) / denominator

    def multiply(item):
        line, within = lax.div(item, group), lax.rem(item, group)
        step, sub = lax.div(within, SUBS), lax.rem(within, SUBS)

        @pl.when(within == 0)
        def _():
            begin_line(line)

        def term(way, position):
            owner = ring_owner(lax.rem(position + count, count), count)
            columns = pl.ds(pl.multiple_of(lax.rem(owner, per) * depth + way * half, half), half)
            return jnp.dot(
                panel[lax.div(owner, per), :, columns], land[way, item], preferred_element_type=jnp.float32
            )

        place_columns = pl.ds(pl.multiple_of(sub * width, width), width)
        total[:, place_columns] += term(0, place - step) + term(1, place + step)

        @pl.when(within == group - 1)
        def _():
            @pl.when(line < lines - 1)
            def _():
                end_line(line)

            write_line(line).start()

    def arrive(event):
        line = lax.div(event, group - SUBS)
        slot = event + SUBS * (line + 1)
        last = lax.rem(slot, group) >= group - SUBS
        source = jnp.where(last, slot + SUBS, slot)
        for way in range(2):
            hop(way, land.at[way, slot], slot).wait_recv()

            @pl.when(source + SUBS < slots)
            def _():
                hop(way, land.at[way, source], source + SUBS).start()

    @pl.loop(0, events)
    def _(event):
        @pl.when(event == start * 3 // 4)
        def _():
            for k in range(1, chips):
                origin = from_chip(k)
                w_copy(2 * k - 1, panel.at[origin], origin, sibling).wait_recv()
                w_copy(2 * k, panel.at[origin], origin, sibling).start()

        @pl.when(event == start)
        def _():
            w_copy(0, interaction, sibling, sibling).wait_recv()
            for k in range(1, chips):
                origin = lax.rem(sibling + cols - 2 * k, cols)
                w_copy(2 * k, panel.at[origin], origin, sibling).wait_recv()

        @pl.loop(0, 2)
        def _(which):
            @pl.when(event >= start)
            def _():
                multiply(2 * (event - start) + which)

            @pl.when(which == 0)
            def _():
                arrive(event)

    write_line(lines - 1).wait()

    @pl.loop(0, events)
    def _(event):
        slot = event + SUBS * (lax.div(event, group - SUBS) + 1)
        for way in range(2):
            hop(way, land.at[way, slot], slot).wait_send()

    w_copy(0, interaction, col, sibling).wait_send()
    for k in range(1, chips):
        w_copy(2 * k - 1, interaction, col, sibling).wait_send()
        origin = from_chip(k)
        w_copy(2 * k, panel.at[origin], origin, sibling).wait_send()


def finish_kernel(mixed, dressing, row_energy, column_energy, out):
    orbitals = dressing.shape[0]
    done = out.shape[1] - orbitals
    if done:
        out[:, :done] = mixed[:, :done]
    summed = mixed[:, done:]
    denominator = row_energy[...] + column_energy[...]
    first_order = (summed / denominator).astype(jnp.bfloat16)
    dressed = jnp.dot(first_order, dressing[...], preferred_element_type=jnp.float32).astype(jnp.bfloat16)
    out[:, done:] = (summed + dressed.astype(jnp.float32)) / denominator


def finish_last(mixed, dressing, row_energy, column_energy):
    rows, columns = mixed.shape
    orbitals = dressing.shape[0]
    tile = rows // 8
    return pl.pallas_call(
        finish_kernel,
        out_shape=jax.ShapeDtypeStruct((rows, columns), jnp.float32),
        grid=(rows // tile,),
        in_specs=[
            pl.BlockSpec((tile, columns), lambda i: (i, 0)),
            pl.BlockSpec((orbitals, orbitals), lambda i: (0, 0)),
            pl.BlockSpec((tile, 1), lambda i: (i, 0)),
            pl.BlockSpec((1, orbitals), lambda i: (0, 0)),
        ],
        out_specs=pl.BlockSpec((tile, columns), lambda i: (i, 0)),
        compiler_params=pltpu.CompilerParams(vmem_limit_bytes=60 * 1024 * 1024),
        cost_estimate=pl.CostEstimate(
            flops=2 * rows * orbitals * orbitals, bytes_accessed=8 * rows * columns, transcendentals=0
        ),
    )(mixed, dressing, row_energy, column_energy)


def whole_lines(mesh, interaction, amplitudes, driver, dressing, row_energy, column_energy):
    count, cols = mesh.shape["row"], mesh.shape["col"]
    rows, columns = driver.shape
    depth = amplitudes.shape[0]
    orbitals = dressing.shape[0]
    lines = columns // orbitals
    slots = lines * count * SUBS
    dma = pltpu.SemaphoreType.DMA
    anywhere = pl.BlockSpec(memory_space=pl.ANY)
    vmem = pl.BlockSpec(memory_space=pltpu.VMEM)
    row_energy = row_energy[:, None]
    column_energy = column_energy.reshape(lines, orbitals)
    mixed = pl.pallas_call(
        functools.partial(ring_kernel, count, cols, lines),
        out_shape=jax.ShapeDtypeStruct((rows, columns), jnp.float32),
        in_specs=[anywhere] * 4 + [vmem] * 2,
        out_specs=anywhere,
        scratch_shapes=[
            pltpu.VMEM((2, slots, depth // 2, orbitals // SUBS), jnp.bfloat16),
            pltpu.VMEM((cols,) + interaction.shape, jnp.bfloat16),
            pltpu.VMEM((rows, orbitals), jnp.float32),
            pltpu.VMEM((rows, orbitals), jnp.bfloat16),
            pltpu.VMEM(dressing.shape, jnp.bfloat16),
            dma((2, slots)),
            dma((2, slots)),
            dma((cols - 1,)),
            dma((cols - 1,)),
            dma((2, lines * SUBS)),
            dma((4,)),
        ],
        compiler_params=pltpu.CompilerParams(
            collective_id=0, has_side_effects=True, vmem_limit_bytes=62 * 1024 * 1024
        ),
        cost_estimate=pl.CostEstimate(
            flops=2 * rows * columns * (depth * count + orbitals), bytes_accessed=2 * rows * columns * 10, transcendentals=0
        ),
    )(amplitudes, interaction, driver, dressing, row_energy, column_energy)
    return finish_last(mixed, dressing, row_energy, column_energy[lines - 1 :])


def solution(mesh):
    count = mesh.shape["row"]

    def on_device(interaction, amplitudes, driver, dressing, occ_energy, vir_energy):
        row_count, column_count = driver.shape
        row_energy = line_energy(occ_energy, vir_energy, lax.axis_index("row") * row_count, row_count)
        column_energy = line_energy(occ_energy, vir_energy, lax.axis_index("col") * column_count, column_count)
        if column_count % dressing.shape[0] == 0:
            return whole_lines(mesh, interaction, amplitudes, driver, dressing, row_energy, column_energy)
        cycle_term = cycle(interaction, amplitudes, count)
        denominator = row_energy[:, None] + column_energy[None, :]
        summed = driver.astype(jnp.float32) + cycle_term
        first_order = (summed / denominator).astype(jnp.bfloat16)
        dressed = dress(first_order, dressing)
        return (summed + dressed.astype(jnp.float32)) / denominator

    return jax.shard_map(
        on_device,
        mesh=mesh,
        in_specs=(P("row", "col"), P("row", "col"), P("row", "col"), P(), P(), P()),
        out_specs=P("row", "col"),
        check_vma=False,
    )
```

```python
import functools

import jax
import jax.numpy as jnp
from jax import lax
from jax.experimental import pallas as pl
from jax.experimental.pallas import tpu as pltpu
from jax.sharding import PartitionSpec as P


def ring_owner(position, count):
    return jnp.where(position < count // 2, 2 * position, 2 * (count - 1 - position) + 1)


def ring_position(index, count):
    return jnp.where(index % 2 == 0, index // 2, count - 1 - index // 2)


def line_energy(occupied, virtual, offset, length):
    orbitals = virtual.shape[0]
    energy = jnp.repeat(occupied, orbitals) - jnp.tile(virtual, occupied.shape[0])
    return lax.dynamic_slice_in_dim(energy, offset, length)


def dress(first_order, dressing):
    orbitals = dressing.shape[0]
    rows, columns = first_order.shape
    if columns % orbitals == 0:
        parts = [
            jnp.dot(first_order[:, j : j + orbitals], dressing, preferred_element_type=jnp.float32).astype(jnp.bfloat16)
            for j in range(0, columns, orbitals)
        ]
        return jnp.concatenate(parts, axis=1)
    lines = lax.all_to_all(first_order, "col", split_axis=0, concat_axis=1, tiled=True)
    line_rows, line_columns = lines.shape
    flattened = lines.reshape(line_rows * (line_columns // orbitals), orbitals)
    dressed_lines = jnp.dot(flattened, dressing, preferred_element_type=jnp.float32)
    dressed_lines = dressed_lines.reshape(line_rows, line_columns).astype(jnp.bfloat16)
    return lax.all_to_all(dressed_lines, "col", split_axis=1, concat_axis=0, tiled=True)


def cycle(interaction, amplitudes, count):
    order = list(range(0, count, 2)) + list(range(count - 1, 0, -2))
    up = [(order[p], order[(p + 1) % count]) for p in range(count)]
    down = [(b, a) for a, b in up]
    panel = lax.all_gather(interaction, "col", axis=1, tiled=True)
    depth = amplitudes.shape[0]
    half = depth // 2
    place = ring_position(lax.axis_index("row"), count)
    total = None
    waiting = []
    high, low = amplitudes[:half], amplitudes[half:]
    for step in range(count):
        if step < count - 1:
            next_high = lax.ppermute(high, "row", up)
            next_low = lax.ppermute(low, "row", down)
        waiting += [(high, place - step, 0), (low, place + step, half)]
        for block, position, shift in waiting if step >= 2 else ():
            owner = ring_owner((position + count) % count, count)
            part = lax.dynamic_slice_in_dim(panel, owner * depth + shift, half, axis=1)
            term = jnp.dot(part, block, preferred_element_type=jnp.float32)
            total = term if total is None else total + term
        if step >= 2:
            waiting = []
            next_high, next_low, total = lax.optimization_barrier((next_high, next_low, total))
        else:
            next_high, next_low = lax.optimization_barrier((next_high, next_low))
        high, low = next_high, next_low
    return total


MESH = pl.DeviceIdType.MESH
SUBS = 4


def energy_sum(occ_energy, vir_energy, first_row, tile, line):
    orbitals = vir_energy.shape[1]
    start = pl.multiple_of(lax.rem(first_row, orbitals), tile)
    across = jnp.broadcast_to(vir_energy[:, pl.ds(start, tile)], (128, tile))
    row_energy = occ_energy[lax.div(first_row, orbitals)] - across.T[:, :1]
    column_energy = occ_energy[line] - vir_energy[...]
    return row_energy + column_energy


def ring_kernel(
    count, cols, lines, amplitudes, interaction, driver, dressing, occ_energy, vir_energy, out,
    land, panel, total, driver_line, operator, send_sem, recv_sem, w_send, w_recv, own_sem, local_sem,
):
    row, col = lax.axis_index("row"), lax.axis_index("col")
    place = jnp.where(lax.rem(row, 2) == 0, lax.div(row, 2), count - 1 - lax.div(row, 2))
    up = ring_owner(lax.rem(place + 1, count), count)
    down = ring_owner(lax.rem(place + count - 1, count), count)
    sibling = col + 1 - 2 * lax.rem(col, 2)
    half, width = land.shape[2], land.shape[3]
    depth = 2 * half
    per = panel.shape[2] // depth
    orbitals = operator.shape[0]
    group = count * SUBS
    slots = lines * group
    chips = cols // 2
    events = slots - lines * SUBS
    start = events - slots // 2

    barrier = pltpu.get_barrier_semaphore()
    partners = [(up, col), (down, col), (row, sibling)]
    partners += [(row, lax.rem(col + 2 * k, cols)) for k in range(1, chips)]
    for partner in partners:
        pl.semaphore_signal(barrier, inc=1, device_id=partner, device_id_type=MESH)
    pl.semaphore_wait(barrier, len(partners))

    def hop(way, source, slot):
        return pltpu.make_async_remote_copy(
            src_ref=source, dst_ref=land.at[way, slot], send_sem=send_sem.at[way, slot],
            recv_sem=recv_sem.at[way, slot], device_id=((up, down)[way], col), device_id_type=MESH,
        )

    def own_block(way, line, sub):
        return amplitudes.at[pl.ds(way * half, half), pl.ds(line * orbitals + sub * width, width)]

    for sub in range(SUBS):
        for way in range(2):
            hop(way, own_block(way, 0, sub), SUBS + sub).start()

    def w_copy(index, source, slot, target):
        return pltpu.make_async_remote_copy(
            src_ref=source, dst_ref=panel.at[slot], send_sem=w_send.at[index],
            recv_sem=w_recv.at[index], device_id=(row, target), device_id_type=MESH,
        )

    def from_chip(k):
        return lax.rem(col + cols - 2 * k, cols)

    for k in range(1, chips):
        w_copy(2 * k - 1, interaction, col, lax.rem(col + 2 * k, cols)).start()
    w_copy(0, interaction, col, sibling).start()

    own_copies = [
        pltpu.make_async_copy(own_block(way, line, sub), land.at[way, line * group + sub], own_sem.at[way, line * SUBS + sub])
        for line in range(lines) for sub in range(SUBS) for way in range(2)
    ]
    own_copies.append(pltpu.make_async_copy(interaction, panel.at[col], local_sem.at[0]))
    own_copies.append(pltpu.make_async_copy(dressing, operator, local_sem.at[1]))
    for copy in own_copies:
        copy.start()

    def load_driver(line):
        return pltpu.make_async_copy(
            driver.at[:, pl.ds(pl.multiple_of(line * orbitals, orbitals), orbitals)], driver_line, local_sem.at[2]
        )

    def write_line(line):
        return pltpu.make_async_copy(
            total, out.at[:, pl.ds(pl.multiple_of(line * orbitals, orbitals), orbitals)], local_sem.at[3]
        )

    load_driver(0).start()
    for copy in own_copies:
        copy.wait()

    def begin_line(line):
        @pl.when(line > 0)
        def _():
            write_line(line - 1).wait()

        load_driver(line).wait()
        total[...] = driver_line[...].astype(jnp.float32)

        @pl.when(line + 1 < lines)
        def _():
            load_driver(line + 1).start()

    tile = total.shape[0] // 4

    def end_line(line):
        @pl.loop(0, 4)
        def _(index):
            rows = pl.ds(pl.multiple_of(index * tile, tile), tile)
            summed = total[rows, :]
            denominator = energy_sum(
                occ_energy, vir_energy, row * total.shape[0] + index * tile, tile, col * lines + line
            )
            first_order = (summed / denominator).astype(jnp.bfloat16)
            dressed = jnp.dot(first_order, operator[...], preferred_element_type=jnp.float32).astype(jnp.bfloat16)
            total[rows, :] = (summed + dressed.astype(jnp.float32)) / denominator

    def multiply(item):
        line, within = lax.div(item, group), lax.rem(item, group)
        step, sub = lax.div(within, SUBS), lax.rem(within, SUBS)

        @pl.when(within == 0)
        def _():
            begin_line(line)

        def term(way, position):
            owner = ring_owner(lax.rem(position + count, count), count)
            columns = pl.ds(pl.multiple_of(lax.rem(owner, per) * depth + way * half, half), half)
            return jnp.dot(
                panel[lax.div(owner, per), :, columns], land[way, item], preferred_element_type=jnp.float32
            )

        place_columns = pl.ds(pl.multiple_of(sub * width, width), width)
        total[:, place_columns] += term(0, place - step) + term(1, place + step)

        @pl.when(within == group - 1)
        def _():
            @pl.when(line < lines - 1)
            def _():
                end_line(line)

            write_line(line).start()

    def arrive(event):
        line = lax.div(event, group - SUBS)
        slot = event + SUBS * (line + 1)
        last = lax.rem(slot, group) >= group - SUBS
        source = jnp.where(last, slot + SUBS, slot)
        for way in range(2):
            hop(way, land.at[way, slot], slot).wait_recv()

            @pl.when(source + SUBS < slots)
            def _():
                hop(way, land.at[way, source], source + SUBS).start()

    @pl.loop(0, events)
    def _(event):
        @pl.when(event == start * 3 // 4)
        def _():
            for k in range(1, chips):
                origin = from_chip(k)
                w_copy(2 * k - 1, panel.at[origin], origin, sibling).wait_recv()
                w_copy(2 * k, panel.at[origin], origin, sibling).start()

        @pl.when(event == start)
        def _():
            w_copy(0, interaction, sibling, sibling).wait_recv()
            for k in range(1, chips):
                origin = lax.rem(sibling + cols - 2 * k, cols)
                w_copy(2 * k, panel.at[origin], origin, sibling).wait_recv()

        @pl.loop(0, 2)
        def _(which):
            @pl.when(event >= start)
            def _():
                multiply(2 * (event - start) + which)

            @pl.when(which == 0)
            def _():
                arrive(event)

    write_line(lines - 1).wait()

    @pl.loop(0, events)
    def _(event):
        slot = event + SUBS * (lax.div(event, group - SUBS) + 1)
        for way in range(2):
            hop(way, land.at[way, slot], slot).wait_send()

    w_copy(0, interaction, col, sibling).wait_send()
    for k in range(1, chips):
        w_copy(2 * k - 1, interaction, col, sibling).wait_send()
        origin = from_chip(k)
        w_copy(2 * k, panel.at[origin], origin, sibling).wait_send()


def finish_kernel(lines, grid, mixed, dressing, occ_energy, vir_energy, out):
    tile = mixed.shape[0]
    orbitals = dressing.shape[0]
    done = out.shape[1] - orbitals
    if done:
        out[:, :done] = mixed[:, :done]
    summed = mixed[:, done:]
    first_row = (lax.axis_index("row") * grid + pl.program_id(0)) * tile
    line = lax.axis_index("col") * lines + lines - 1
    denominator = energy_sum(occ_energy, vir_energy, first_row, tile, line)
    first_order = (summed / denominator).astype(jnp.bfloat16)
    dressed = jnp.dot(first_order, dressing[...], preferred_element_type=jnp.float32).astype(jnp.bfloat16)
    out[:, done:] = (summed + dressed.astype(jnp.float32)) / denominator


def finish_last(mixed, dressing, occ_energy, vir_energy):
    rows, columns = mixed.shape
    orbitals = dressing.shape[0]
    tile = rows // 4
    return pl.pallas_call(
        functools.partial(finish_kernel, columns // orbitals, rows // tile),
        out_shape=jax.ShapeDtypeStruct((rows, columns), jnp.float32),
        grid=(rows // tile,),
        in_specs=[
            pl.BlockSpec((tile, columns), lambda i: (i, 0)),
            pl.BlockSpec((orbitals, orbitals), lambda i: (0, 0)),
            pl.BlockSpec(memory_space=pltpu.SMEM),
            pl.BlockSpec((1, orbitals), lambda i: (0, 0)),
        ],
        out_specs=pl.BlockSpec((tile, columns), lambda i: (i, 0)),
        compiler_params=pltpu.CompilerParams(vmem_limit_bytes=60 * 1024 * 1024),
        cost_estimate=pl.CostEstimate(
            flops=2 * rows * orbitals * orbitals, bytes_accessed=8 * rows * columns, transcendentals=0
        ),
    )(mixed, dressing, occ_energy, vir_energy)


def whole_lines(mesh, interaction, amplitudes, driver, dressing, occ_energy, vir_energy):
    count, cols = mesh.shape["row"], mesh.shape["col"]
    rows, columns = driver.shape
    depth = amplitudes.shape[0]
    orbitals = dressing.shape[0]
    lines = columns // orbitals
    slots = lines * count * SUBS
    dma = pltpu.SemaphoreType.DMA
    anywhere = pl.BlockSpec(memory_space=pl.ANY)
    vmem = pl.BlockSpec(memory_space=pltpu.VMEM)
    vir_energy = vir_energy[None, :]
    mixed = pl.pallas_call(
        functools.partial(ring_kernel, count, cols, lines),
        out_shape=jax.ShapeDtypeStruct((rows, columns), jnp.float32),
        in_specs=[anywhere] * 4 + [pl.BlockSpec(memory_space=pltpu.SMEM), vmem],
        out_specs=anywhere,
        scratch_shapes=[
            pltpu.VMEM((2, slots, depth // 2, orbitals // SUBS), jnp.bfloat16),
            pltpu.VMEM((cols,) + interaction.shape, jnp.bfloat16),
            pltpu.VMEM((rows, orbitals), jnp.float32),
            pltpu.VMEM((rows, orbitals), jnp.bfloat16),
            pltpu.VMEM(dressing.shape, jnp.bfloat16),
            dma((2, slots)),
            dma((2, slots)),
            dma((cols - 1,)),
            dma((cols - 1,)),
            dma((2, lines * SUBS)),
            dma((4,)),
        ],
        compiler_params=pltpu.CompilerParams(
            collective_id=0, has_side_effects=True, vmem_limit_bytes=62 * 1024 * 1024
        ),
        cost_estimate=pl.CostEstimate(
            flops=2 * rows * columns * (depth * count + orbitals), bytes_accessed=2 * rows * columns * 10, transcendentals=0
        ),
    )(amplitudes, interaction, driver, dressing, occ_energy, vir_energy)
    return finish_last(mixed, dressing, occ_energy, vir_energy)


def solution(mesh):
    count = mesh.shape["row"]

    def on_device(interaction, amplitudes, driver, dressing, occ_energy, vir_energy):
        row_count, column_count = driver.shape
        row_energy = line_energy(occ_energy, vir_energy, lax.axis_index("row") * row_count, row_count)
        column_energy = line_energy(occ_energy, vir_energy, lax.axis_index("col") * column_count, column_count)
        if column_count % dressing.shape[0] == 0:
            return whole_lines(mesh, interaction, amplitudes, driver, dressing, occ_energy, vir_energy)
        cycle_term = cycle(interaction, amplitudes, count)
        denominator = row_energy[:, None] + column_energy[None, :]
        summed = driver.astype(jnp.float32) + cycle_term
        first_order = (summed / denominator).astype(jnp.bfloat16)
        dressed = dress(first_order, dressing)
        return (summed + dressed.astype(jnp.float32)) / denominator

    return jax.shard_map(
        on_device,
        mesh=mesh,
        in_specs=(P("row", "col"), P("row", "col"), P("row", "col"), P(), P(), P()),
        out_specs=P("row", "col"),
        check_vma=False,
    )
```
